256 devices in a mesh: ctx: 64 (over z, x_hi, y), head: 4 (over x_lo, core).
Axes of the slice: x: 4 (x_hi: 2, x_lo: 2; x = x_hi * 2 + x_lo), y: 4, z: 8, core: 2. Of those that a mesh axis runs over, the one named last changes fastest.
Arguments:
- queries: bfloat16 [32768, 8192], P(('ctx', 'head')), may hold values from -80 to 80
- key_vectors: bfloat16 [32768, 1024], P(('ctx', 'head')), may hold values from -4 to 4
- value_vectors: bfloat16 [32768, 1024], P(('ctx', 'head')), may hold values from -6 to 6
- out_grad: bfloat16 [32768, 8192], P(('ctx', 'head')), may hold values from -6 to 6
- doc_starts: int32 [127], replicated, may hold values from 2 to 32766, as said below
Outputs:
- grad_query: bfloat16 [32768, 8192], P(('ctx', 'head'))
- grad_key: bfloat16 [32768, 1024], P(('ctx', 'head'))
- grad_value: bfloat16 [32768, 1024], P(('ctx', 'head'))
The draws below stay inside these ranges and needn't reach their ends.
Inputs may be any that keep to these rules, and one draw needn't show every extreme that they name: `doc_starts`: increasing and even; every document, the first and last too, holds at most 510 tokens, and one holds exactly 510.
All inputs are finite; a program needn't handle non-finite values.
Results may differ from the reference program's by a relative error of at most 0.012.
Values may be sent and summed in bfloat16 or wider, within the bound.
No kernel may reach another device: no remote copies, remote signals or barrier semaphores. Data moves between devices by JAX's collectives and lax.ppermute only.
A program may use at most 192 MiB of HBM per device.

```python
import math
import jax
import jax.numpy as jnp
from jax import lax

HD = 128
QH = 64
KVH = 8
TOK_DEV = 512
TOKENS = 32768
HOPS = 1
DOCS = 127
N_CTX = 64


def base_keys(key):
    return jnp.clip(jax.random.normal(key, (TOKENS, KVH, HD), jnp.float32), -4.0, 4.0)


def draw_key_vectors(key, part):
    shared = base_keys(key)
    result = shared
    return result.reshape(TOKENS, KVH * HD).astype(jnp.bfloat16)


def draw_queries(key, part):
    key = jax.random.fold_in(key, 7)
    result = jnp.clip(jax.random.normal(key, (TOKENS, QH * HD), jnp.float32), -4.0, 4.0)
    return result.astype(jnp.bfloat16)


def draw_doc_starts(key, part):
    key = jax.random.fold_in(key, 3)
    half = TOK_DEV * HOPS // 2
    first_key, second_key = jax.random.split(key)
    offsets = 2 * jax.random.randint(first_key, (DOCS,), 0, half // 2)
    picked = jax.random.randint(second_key, (), 0, DOCS - 1)
    index = jnp.arange(DOCS, dtype=jnp.int32)
    offsets = jnp.where(index == picked, 0, offsets)
    offsets = jnp.where(index == picked + 1, half - 2, offsets)
    return ((index + 1) * half + offsets).astype(jnp.int32)


def level_of(stream_key, dims, shards, low, largest):
    loudness, own = 1.0, jax.random.fold_in(stream_key, 6)
    for axis_at, parts in shards:
        steps = jnp.exp(jax.random.uniform(jax.random.fold_in(own, axis_at), (parts,), jnp.float32, low / len(shards), largest / len(shards)))
        loudness = loudness * jnp.repeat(steps, dims[axis_at] // parts).reshape([-1 if axis == axis_at else 1 for axis in range(len(dims))])
    return loudness


def normal_values(rng, shape, width, reach, cuts=(), kind=jnp.bfloat16):
    loudness = level_of(rng, shape, cuts, -0.22, 0.18) if cuts else 1.0
    entries = jax.random.normal(rng, shape, jnp.float32) * width * loudness
    return jnp.minimum(jnp.maximum(entries, -reach), reach).astype(kind)


def setup_inputs(seed: int = 0) -> dict:
    splits = jax.random.split(jax.random.key(seed), 6)
    return {
        "queries": draw_queries(jax.random.fold_in(splits[5], 71), 0),
        "key_vectors": draw_key_vectors(jax.random.fold_in(splits[5], 71), 0),
        "value_vectors": normal_values(splits[2], (TOKENS, KVH * HD), 1.0, 6.0, ((0, 256),)),
        "out_grad": normal_values(splits[3], (TOKENS, QH * HD), 1.0, 6.0, ((0, 256),)),
        "doc_starts": draw_doc_starts(jax.random.fold_in(splits[5], 71), 0),
    }


NEG_FILL = -1e+30

def to_wide(values):
    return values.astype(jnp.float32)

def rounded(values):
    low = lax.optimization_barrier(values.astype(jnp.bfloat16))
    return low.astype(jnp.float32)

def segment_of(positions, doc_starts):
    return lax.optimization_barrier(jnp.sum((doc_starts[None, :] <= positions[:, None]).astype(jnp.int32), axis=1))

def reference(queries, key_vectors, value_vectors, out_grad, doc_starts):
    group = QH // KVH
    scale = 1.0 / math.sqrt(HD)
    margin = HOPS * TOK_DEV
    window = (HOPS + 1) * TOK_DEV
    query_split = queries.reshape(TOKENS, KVH, group, HD)
    grad_split = out_grad.reshape(TOKENS, KVH, group, HD)
    key_split = key_vectors.reshape(TOKENS, KVH, HD)
    value_split = value_vectors.reshape(TOKENS, KVH, HD)
    key_pad = jnp.concatenate([jnp.zeros((margin, KVH, HD), key_vectors.dtype), key_split], axis=0)
    value_pad = jnp.concatenate([jnp.zeros((margin, KVH, HD), value_vectors.dtype), value_split], axis=0)

    def query_block(block):
        start = (block * TOK_DEV).astype(jnp.int32)
        query_pos = start + jnp.arange(TOK_DEV, dtype=jnp.int32)
        key_pos = start - margin + jnp.arange(window, dtype=jnp.int32)
        allowed = (key_pos[None, :] >= 0) & (key_pos[None, :] <= query_pos[:, None])
        allowed = allowed & (segment_of(query_pos, doc_starts)[:, None] == segment_of(key_pos, doc_starts)[None, :])
        query_blk = lax.dynamic_slice_in_dim(query_split, start, TOK_DEV, 0)
        grad_blk = lax.dynamic_slice_in_dim(grad_split, start, TOK_DEV, 0)
        key_blk = lax.dynamic_slice_in_dim(key_pad, start, window, 0)
        value_blk = lax.dynamic_slice_in_dim(value_pad, start, window, 0)
        scores = jnp.einsum('pkgd,tkd->kgpt', to_wide(query_blk), to_wide(key_blk)) * scale
        scores = jnp.where(allowed[None, None], scores, NEG_FILL)
        top = lax.optimization_barrier(jnp.max(scores, axis=-1))
        weights = jnp.where(allowed[None, None], jnp.exp(scores - top[..., None]), 0.0)
        log_total = top + jnp.log(lax.optimization_barrier(jnp.sum(weights, axis=-1)))
        probs = jnp.where(allowed[None, None], jnp.exp(scores - log_total[..., None]), 0.0)
        dprobs = jnp.einsum('pkgd,tkd->kgpt', to_wide(grad_blk), to_wide(value_blk))
        delta = lax.optimization_barrier(jnp.sum(probs * dprobs, axis=-1))
        dscores = rounded(probs * (dprobs - delta[..., None]))
        grad_q = jnp.einsum('kgpt,tkd->pkgd', dscores, to_wide(key_blk)) * scale
        return (grad_q.astype(jnp.bfloat16), log_total, delta)
    grad_blocks, log_totals, deltas = lax.map(query_block, jnp.arange(N_CTX, dtype=jnp.int32))
    grad_query = grad_blocks.reshape(TOKENS, QH * HD)
    lse_all = jnp.transpose(log_totals, (1, 2, 0, 3)).reshape(KVH, group, TOKENS)
    delta_all = jnp.transpose(deltas, (1, 2, 0, 3)).reshape(KVH, group, TOKENS)
    query_pad = jnp.concatenate([query_split, jnp.zeros((margin, KVH, group, HD), queries.dtype)], axis=0)
    grad_pad = jnp.concatenate([grad_split, jnp.zeros((margin, KVH, group, HD), out_grad.dtype)], axis=0)
    lse_pad = jnp.concatenate([lse_all, jnp.zeros((KVH, group, margin), jnp.float32)], axis=2)
    delta_pad = jnp.concatenate([delta_all, jnp.zeros((KVH, group, margin), jnp.float32)], axis=2)

    def key_block(block):
        start = (block * TOK_DEV).astype(jnp.int32)
        key_pos = start + jnp.arange(TOK_DEV, dtype=jnp.int32)
        query_pos = start + jnp.arange(window, dtype=jnp.int32)
        allowed = (query_pos[:, None] < TOKENS) & (key_pos[None, :] <= query_pos[:, None])
        allowed = allowed & (segment_of(query_pos, doc_starts)[:, None] == segment_of(key_pos, doc_starts)[None, :])
        query_blk = lax.dynamic_slice_in_dim(query_pad, start, window, 0)
        grad_blk = lax.dynamic_slice_in_dim(grad_pad, start, window, 0)
        lse_blk = lax.dynamic_slice_in_dim(lse_pad, start, window, 2)
        delta_blk = lax.dynamic_slice_in_dim(delta_pad, start, window, 2)
        key_blk = lax.dynamic_slice_in_dim(key_split, start, TOK_DEV, 0)
        value_blk = lax.dynamic_slice_in_dim(value_split, start, TOK_DEV, 0)
        scores = jnp.einsum('pkgd,tkd->kgpt', to_wide(query_blk), to_wide(key_blk)) * scale
        scores = jnp.where(allowed[None, None], scores, NEG_FILL)
        probs = jnp.where(allowed[None, None], jnp.exp(scores - lse_blk[..., None]), 0.0)
        dprobs = jnp.einsum('pkgd,tkd->kgpt', to_wide(grad_blk), to_wide(value_blk))
        dscores = rounded(probs * (dprobs - delta_blk[..., None]))
        grad_k = jnp.einsum('kgpt,pkgd->tkd', dscores, to_wide(query_blk)) * scale
        grad_v = jnp.einsum('kgpt,pkgd->tkd', rounded(probs), to_wide(grad_blk))
        return (grad_k.astype(jnp.bfloat16), grad_v.astype(jnp.bfloat16))
    key_grads, value_grads = lax.map(key_block, jnp.arange(N_CTX, dtype=jnp.int32))
    grad_key = key_grads.reshape(TOKENS, KVH * HD)
    grad_value = value_grads.reshape(TOKENS, KVH * HD)
    return (grad_query, grad_key, grad_value)
```

```python
import functools, math
import jax, jax.numpy as jnp
from jax import lax
from jax.experimental import pallas as pl
from jax.experimental.pallas import tpu as pltpu
from jax.sharding import PartitionSpec as P
HD=128; BLK=128; GRP=8; WIN=640
SCALE=1.0/math.sqrt(HD); LOG2E=1.4426950408889634
TT=(((1,),(1,)),((),()))
NN=(((1,),(0,)),((),()))
TN=(((0,),(0,)),((),()))
f32=jnp.float32; bf16=jnp.bfloat16

def kernel(scal, first_ref, qa, qb, ga, gb, y_ref, x_ref, o_ref, *rest, pair, mode):
    dqa, dqb, dy, dx, do, kv, bias, pt, dst, acc = rest[-10:]
    j = pl.program_id(0)
    off_a = pl.multiple_of(scal[1]*BLK, BLK)
    off_b = pl.multiple_of((1-scal[1])*BLK, BLK)
    kv[0:256] = y_ref[...]; kv[256:512]=x_ref[...]; kv[512:768]=o_ref[...]
    @pl.when(j==0)
    def _():
        for s, off in ((0,off_a),(1,off_b)):
            t = lax.broadcasted_iota(jnp.int32,(WIN,BLK),0)+off
            p = lax.broadcasted_iota(jnp.int32,(WIN,BLK),1)+off+512
            ok = (t<=p)&(t>=first_ref[s:s+1,:])
            bias[s]=jnp.where(ok,0.0,-1e30).astype(f32)
    acc[...]=jnp.zeros_like(acc)
    for s,(q,g,dq,off) in enumerate(((qa,ga,dqa,off_a),(qb,gb,dqb,off_b))):
        K=kv[pl.ds(off,WIN),0:128]; V=kv[pl.ds(off,WIN),128:256]
        KT=K.T
        for i in range(0,GRP,pair):
            cols=[slice((i+u)*HD,(i+u+1)*HD) for u in range(pair)]
            Q=jnp.concatenate([q[:,c] for c in cols],axis=0)
            G=jnp.concatenate([g[:,c] for c in cols],axis=0)
            S=lax.dot_general(K,Q,TT,preferred_element_type=f32)
            D=lax.dot_general(V,G,TT,preferred_element_type=f32)
            b=bias[s]
            b=jnp.concatenate([b]*pair,axis=1)
            u=S*(SCALE*LOG2E)+b
            m=jnp.max(u,axis=0,keepdims=True)
            e=jnp.exp2(u-m)
            l=jnp.sum(e,axis=0,keepdims=True)
            w=jnp.sum(e*D,axis=0,keepdims=True)
            r=1.0/l
            dl=w*r
            Pm=e*r
            dS=(Pm*(D-dl)).astype(bf16)
            Pl=Pm.astype(bf16)
            w0=i*HD
            pt[:,w0:w0+pair*HD]=Pl
            dst[:,w0:w0+pair*HD]=dS
            if mode==0:
                dQT=lax.dot_general(KT,dS,NN,preferred_element_type=f32)
                for uu,c in enumerate(cols):
                    dq[:,c]=(dQT[:,uu*HD:(uu+1)*HD].T*SCALE).astype(bf16)
            elif mode==1:
                dQ=lax.dot_general(dS,K,TN,preferred_element_type=f32)*SCALE
                for uu,c in enumerate(cols):
                    dq[:,c]=dQ[uu*HD:(uu+1)*HD].astype(bf16)
        Qf=jnp.concatenate([q[:,i*HD:(i+1)*HD] for i in range(GRP)],axis=0)
        Gf=jnp.concatenate([g[:,i*HD:(i+1)*HD] for i in range(GRP)],axis=0)
        dK=lax.dot_general(dst[...],Qf,NN,preferred_element_type=f32)*SCALE
        dV=lax.dot_general(pt[...],Gf,NN,preferred_element_type=f32)
        acc[pl.ds(off,WIN),0:128]+=dK
        acc[pl.ds(off,WIN),128:256]+=dV
    dy[...]=acc[0:256].astype(bf16); dx[...]=acc[256:512].astype(bf16); do[...]=acc[512:768]

def chunk(scal, first, q, g, qr, gr, Y, X, O, c0, nk, prev=None, pair=2, mode=0):
    wide=GRP*HD
    own=lambda j,s:(0,s[0]+c0+j)
    oth=lambda j,s:(0,c0+j)
    kvm=lambda j,s:(0,j)
    in_specs=[pl.BlockSpec((2,BLK),lambda j,s:(0,0)),
      pl.BlockSpec((BLK,wide),own),pl.BlockSpec((BLK,wide),oth),
      pl.BlockSpec((BLK,wide),own),pl.BlockSpec((BLK,wide),oth)]+[pl.BlockSpec((256,256),kvm)]*3
    args=[scal,first,q,qr,g,gr,Y,X,O]
    alias={}
    if prev is not None:
        in_specs+=[pl.BlockSpec(memory_space=pl.ANY)]*2
        alias={len(args):0,len(args)+1:1}
        args+=list(prev)
    out_shape=[jax.ShapeDtypeStruct(q.shape,bf16),jax.ShapeDtypeStruct(qr.shape,bf16)]+[jax.ShapeDtypeStruct((256,256*nk),bf16)]*2+[jax.ShapeDtypeStruct((256,256*nk),f32)]
    out_specs=[pl.BlockSpec((BLK,wide),own),pl.BlockSpec((BLK,wide),oth)]+[pl.BlockSpec((256,256),kvm)]*3
    return pl.pallas_call(functools.partial(kernel,pair=pair,mode=mode),
      grid_spec=pltpu.PrefetchScalarGridSpec(num_scalar_prefetch=1,grid=(nk,),in_specs=in_specs,out_specs=out_specs,
        scratch_shapes=[pltpu.VMEM((768,256),bf16),pltpu.VMEM((2,WIN,BLK),f32),pltpu.VMEM((WIN,GRP*HD),bf16),pltpu.VMEM((WIN,GRP*HD),bf16),pltpu.VMEM((768,256),f32)]),
      out_shape=out_shape,input_output_aliases=alias,
      compiler_params=pltpu.CompilerParams(vmem_limit_bytes=48*1024*1024,dimension_semantics=("arbitrary",)),
      cost_estimate=pl.CostEstimate(flops=nk*2*5*2*1024*640*128,bytes_accessed=nk*2*2**20,transcendentals=nk*2*1024*640),
      name="band_grads")(*args)


CHUNKS = (1, 1, 1, 1)
AXES = ("ctx", "head")


def rolled(value, steps):
    count = lax.axis_size("ctx") * lax.axis_size("head")
    return lax.ppermute(value, AXES, [(s, (s + steps) % count) for s in range(count)])


def core_swapped(value):
    count = lax.axis_size("ctx") * lax.axis_size("head")
    return lax.ppermute(value, AXES, [(s, s ^ 1) for s in range(count)])


def kv_half(key_vectors, value_vectors, half):
    width = key_vectors.shape[1] // 2
    k = lax.dynamic_slice_in_dim(key_vectors, half * width, width, 1)
    v = lax.dynamic_slice_in_dim(value_vectors, half * width, width, 1)
    parts = []
    for c in range(0, width, HD):
        parts += [k[:, c : c + HD], v[:, c : c + HD]]
    return jnp.concatenate(parts, axis=1)


def per_device(queries, key_vectors, value_vectors, out_grad, doc_starts):
    head = lax.axis_index("head")
    core = head % 2
    chip = lax.axis_index("ctx") * 2 + head // 2
    mine = kv_half(key_vectors, value_vectors, core)
    theirs = core_swapped(kv_half(key_vectors, value_vectors, 1 - core))
    own = jnp.where(
        core == 0,
        jnp.concatenate([mine, theirs], axis=0),
        jnp.concatenate([theirs, mine], axis=0),
    )
    base = chip * 256 - 512
    rows = jnp.stack([core, 1 - core])[:, None] * BLK + jnp.arange(BLK)[None, :] + chip * 256
    reached = jnp.where(doc_starts[None, None, :] <= rows[:, :, None], doc_starts[None, None, :], 0)
    first = jnp.max(reached, axis=-1) - base
    scal = jnp.stack([core * 4, core])
    half_width = queries.shape[1] // 2
    query_sent = lax.dynamic_slice_in_dim(queries, (1 - core) * half_width, half_width, 1)
    grad_sent = lax.dynamic_slice_in_dim(out_grad, (1 - core) * half_width, half_width, 1)
    query_other = core_swapped(query_sent)
    grad_other = core_swapped(grad_sent)
    offsets = [sum(CHUNKS[:i]) for i in range(len(CHUNKS))]
    moved = []
    for c0, nk in zip(offsets, CHUNKS):
        part = own[:, c0 * 2 * HD : (c0 + nk) * 2 * HD]
        moved.append((rolled(part, 4), rolled(part, 2), part))
    prev = None
    totals = []
    for (c0, nk), (y, x, o) in zip(zip(offsets, CHUNKS), moved):
        dqa, dqb, dy, dx, do = chunk(
            scal, first, queries, out_grad, query_other, grad_other, y, x, o, c0, nk, prev,
            pair=4, mode=0,
        )
        prev = (dqa, dqb)
        total = do + rolled(dx, -2).astype(f32) + rolled(dy, -4).astype(f32)
        totals.append(total.astype(bf16))
    total = jnp.concatenate(totals, axis=1)
    grad_query = lax.dynamic_update_slice_in_dim(
        prev[0], core_swapped(prev[1]), (1 - core) * half_width, 1
    )
    back = core_swapped(lax.dynamic_slice_in_dim(total, (1 - core) * BLK, BLK, 0))
    stay = lax.dynamic_slice_in_dim(total, core * BLK, BLK, 0)
    left = jnp.where(core == 0, stay, back)
    right = jnp.where(core == 0, back, stay)
    heads = [s[:, c : c + HD] for s in (left, right) for c in range(0, s.shape[1], HD)]
    grad_key = jnp.concatenate(heads[0::2], axis=1)
    grad_value = jnp.concatenate(heads[1::2], axis=1)
    return (grad_query, grad_key, grad_value)


def solution(mesh):
    split = P(AXES, None)
    return jax.shard_map(
        per_device,
        mesh=mesh,
        in_specs=(split, split, split, split, P()),
        out_specs=(split, split, split),
        check_vma=False,
    )
```

```python
import functools, math
import jax, jax.numpy as jnp
from jax import lax
from jax.experimental import pallas as pl
from jax.experimental.pallas import tpu as pltpu
from jax.sharding import PartitionSpec as P
HD=128; BLK=128; GRP=8; WIN=640
SCALE=1.0/math.sqrt(HD); LOG2E=1.4426950408889634
TT=(((1,),(1,)),((),()))
NN=(((1,),(0,)),((),()))
TN=(((0,),(0,)),((),()))
f32=jnp.float32; bf16=jnp.bfloat16

def kernel(scal, first_ref, qa, qb, ga, gb, y_ref, x_ref, o_ref, *rest, pair, mode):
    dqa, dqb, dy, dx, do, kv, bias, pt, dst, acc = rest[-10:]
    j = pl.program_id(0)
    off_a = pl.multiple_of(scal[1]*BLK, BLK)
    off_b = pl.multiple_of((1-scal[1])*BLK, BLK)
    kv[0:256] = y_ref[...]; kv[256:512]=x_ref[...]; kv[512:768]=o_ref[...]
    @pl.when(j==0)
    def _():
        for s, off in ((0,off_a),(1,off_b)):
            t = lax.broadcasted_iota(jnp.int32,(WIN,BLK),0)+off
            p = lax.broadcasted_iota(jnp.int32,(WIN,BLK),1)+off+512
            ok = (t<=p)&(t>=first_ref[s:s+1,:])
            bias[s]=jnp.where(ok,0.0,-1e30).astype(f32)
    acc[...]=jnp.zeros_like(acc)
    for s,(q,g,dq,off) in enumerate(((qa,ga,dqa,off_a),(qb,gb,dqb,off_b))):
        K=kv[pl.ds(off,WIN),0:128]; V=kv[pl.ds(off,WIN),128:256]
        KT=K.T
        for i in range(0,GRP,pair):
            cols=[slice((i+u)*HD,(i+u+1)*HD) for u in range(pair)]
            Q=jnp.concatenate([q[:,c] for c in cols],axis=0)
            G=jnp.concatenate([g[:,c] for c in cols],axis=0)
            S=lax.dot_general(K,Q,TT,preferred_element_type=f32)
            D=lax.dot_general(V,G,TT,preferred_element_type=f32)
            b=bias[s]
            b=jnp.concatenate([b]*pair,axis=1)
            u=S*(SCALE*LOG2E)+b
            m=jnp.max(u,axis=0,keepdims=True)
            e=jnp.exp2(u-m)
            l=jnp.sum(e,axis=0,keepdims=True)
            w=jnp.sum(e*D,axis=0,keepdims=True)
            r=1.0/l
            dl=w*r
            Pm=e*r
            dS=(Pm*(D-dl)).astype(bf16)
            Pl=Pm.astype(bf16)
            w0=i*HD
            pt[:,w0:w0+pair*HD]=Pl
            dst[:,w0:w0+pair*HD]=dS
            if mode==0:
                dQT=lax.dot_general(KT,dS,NN,preferred_element_type=f32)
                for uu,c in enumerate(cols):
                    dq[:,c]=(dQT[:,uu*HD:(uu+1)*HD].T*SCALE).astype(bf16)
            elif mode==1:
                dQ=lax.dot_general(dS,K,TN,preferred_element_type=f32)*SCALE
                for uu,c in enumerate(cols):
                    dq[:,c]=dQ[uu*HD:(uu+1)*HD].astype(bf16)
        Qf=jnp.concatenate([q[:,i*HD:(i+1)*HD] for i in range(GRP)],axis=0)
        Gf=jnp.concatenate([g[:,i*HD:(i+1)*HD] for i in range(GRP)],axis=0)
        dK=lax.dot_general(dst[...],Qf,NN,preferred_element_type=f32)*SCALE
        dV=lax.dot_general(pt[...],Gf,NN,preferred_element_type=f32)
        acc[pl.ds(off,WIN),0:128]+=dK
        acc[pl.ds(off,WIN),128:256]+=dV
    dy[...]=acc[0:256].astype(bf16); dx[...]=acc[256:512].astype(bf16); do[...]=acc[512:768]

def chunk(scal, first, q, g, qr, gr, Y, X, O, c0, nk, prev=None, pair=4, mode=0):
    wide=GRP*HD
    own=lambda j,s:(0,s[0]+c0+j)
    oth=lambda j,s:(0,j)
    kvm=lambda j,s:(0,j)
    in_specs=[pl.BlockSpec((2,BLK),lambda j,s:(0,0)),
      pl.BlockSpec((BLK,wide),own),pl.BlockSpec((BLK,wide),own),
      pl.BlockSpec((BLK,wide),own),pl.BlockSpec((BLK,wide),own)]+[pl.BlockSpec((256,256),kvm)]*3
    args=[scal,first,q,qr,g,gr,Y,X,O]
    alias={}
    if prev is not None:
        in_specs+=[pl.BlockSpec(memory_space=pl.ANY)]
        alias={len(args):0}
        args+=[prev]
    out_shape=[jax.ShapeDtypeStruct(q.shape,bf16),jax.ShapeDtypeStruct((BLK,wide*nk),bf16)]+[jax.ShapeDtypeStruct((256,256*nk),bf16)]*2+[jax.ShapeDtypeStruct((256,256*nk),f32)]
    out_specs=[pl.BlockSpec((BLK,wide),own),pl.BlockSpec((BLK,wide),oth)]+[pl.BlockSpec((256,256),kvm)]*3
    return pl.pallas_call(functools.partial(kernel,pair=pair,mode=mode),
      grid_spec=pltpu.PrefetchScalarGridSpec(num_scalar_prefetch=1,grid=(nk,),in_specs=in_specs,out_specs=out_specs,
        scratch_shapes=[pltpu.VMEM((768,256),bf16),pltpu.VMEM((2,WIN,BLK),f32),pltpu.VMEM((WIN,GRP*HD),bf16),pltpu.VMEM((WIN,GRP*HD),bf16),pltpu.VMEM((768,256),f32)]),
      out_shape=out_shape,input_output_aliases=alias,
      compiler_params=pltpu.CompilerParams(vmem_limit_bytes=48*1024*1024,dimension_semantics=("arbitrary",)),
      cost_estimate=pl.CostEstimate(flops=4*nk*2*5*2*1024*640*128,bytes_accessed=nk*2*2**20,transcendentals=0),
      name="band_grads")(*args)


CHUNKS = (2,2)
AXES = ("ctx", "head")
ANY = pl.BlockSpec(memory_space=pl.ANY)


def rolled(value, steps):
    count = lax.axis_size("ctx") * lax.axis_size("head")
    return lax.ppermute(value, AXES, [(s, (s + steps) % count) for s in range(count)])


def core_swapped(value):
    count = lax.axis_size("ctx") * lax.axis_size("head")
    return lax.ppermute(value, AXES, [(s, s ^ 1) for s in range(count)])


def small_call(body, scal, args, in_specs, out_specs, out_shape, alias, name, moved):
    return pl.pallas_call(
        body,
        grid_spec=pltpu.PrefetchScalarGridSpec(
            num_scalar_prefetch=1, grid=(1,), in_specs=in_specs, out_specs=out_specs
        ),
        out_shape=out_shape,
        input_output_aliases=alias,
        compiler_params=pltpu.CompilerParams(vmem_limit_bytes=32 * 1024 * 1024),
        cost_estimate=pl.CostEstimate(flops=0, bytes_accessed=moved, transcendentals=0),
        name=name,
    )(scal, *args)


def assemble(scal, key_vectors, value_vectors, key_other, value_other):
    rows, width = key_vectors.shape
    half = width // 2

    def body(s, km, vm, kt, vt, *outs):
        here = pl.multiple_of(s[1] * rows, rows)
        there = pl.multiple_of((1 - s[1]) * rows, rows)
        c = 0
        for nk, out in zip(CHUNKS, outs):
            for i in range(nk):
                for k, v, at in ((km, vm, here), (kt, vt, there)):
                    out[pl.ds(at, rows), 2 * i * HD : (2 * i + 1) * HD] = k[:, c : c + HD]
                    out[pl.ds(at, rows), (2 * i + 1) * HD : (2 * i + 2) * HD] = v[:, c : c + HD]
                c += HD

    own = pl.BlockSpec((rows, half), lambda j, s: (0, s[1]))
    sizes = [2 * HD * nk for nk in CHUNKS]
    return small_call(
        body, scal, (key_vectors, value_vectors, key_other, value_other), [own] * 4,
        [pl.BlockSpec((2 * rows, size), lambda j, s: (0, 0)) for size in sizes],
        [jax.ShapeDtypeStruct((2 * rows, size), bf16) for size in sizes],
        {}, "assemble", 4 * rows * width * 2,
    )


def add_parts(scal, do, rx, ry, c0, prev):
    size = do.shape[1]
    half = 8 * HD // 2

    def body(s, o, x, y, *rest):
        gk, gv, sent = rest[-3:]
        here = pl.multiple_of(s[1] * BLK, BLK)
        there = pl.multiple_of((1 - s[1]) * BLK, BLK)

        def rows(at):
            return (
                o[pl.ds(at, BLK), :] + x[pl.ds(at, BLK), :].astype(f32) + y[pl.ds(at, BLK), :].astype(f32)
            ).astype(bf16)

        sent[...] = rows(there)
        stay = rows(here)
        for c in range(0, size, 2 * HD):
            gk[:, c // 2 : c // 2 + HD] = stay[:, c : c + HD]
            gv[:, c // 2 : c // 2 + HD] = stay[:, c + HD : c + 2 * HD]

    whole = pl.BlockSpec((2 * BLK, size), lambda j, s: (0, 0))
    per = half * 2 // size
    at = c0 * 2 * HD // size
    out_specs = [pl.BlockSpec((BLK, size // 2), lambda j, s: (0, s[1] * per + at))] * 2
    out_specs += [pl.BlockSpec((BLK, size), lambda j, s: (0, at))]
    shape = jax.ShapeDtypeStruct((BLK, 8 * HD), bf16)
    args, in_specs, alias = (do, rx, ry), [whole] * 3, {}
    if prev is not None:
        args, in_specs, alias = args + tuple(prev), in_specs + [ANY] * 3, {4: 0, 5: 1, 6: 2}
    return small_call(
        body, scal, args, in_specs, out_specs, [shape] * 3, alias, "add_parts", 512 * size * 8
    )


def place_key_grads(scal, gk, gv, back):
    rows, width = back.shape
    half = width // 2

    def body(s, b, k_in, v_in, k_out, v_out):
        for c in range(0, half, HD):
            k_out[:, c : c + HD] = b[:, 2 * c : 2 * c + HD]
            v_out[:, c : c + HD] = b[:, 2 * c + HD : 2 * c + 2 * HD]

    other = pl.BlockSpec((rows, half), lambda j, s: (0, 1 - s[1]))
    shape = jax.ShapeDtypeStruct((rows, width), bf16)
    return small_call(
        body, scal, (back, gk, gv), [pl.BlockSpec((rows, width), lambda j, s: (0, 0)), ANY, ANY],
        [other, other], [shape, shape], {2: 0, 3: 1}, "place_key_grads", 4 * rows * width,
    )


def place_query_grads(scal, dq, backs):
    rows, half = dq.shape[0], dq.shape[1] // 2

    def body(s, *refs):
        out = refs[-1]
        c = 0
        for b in refs[:-2]:
            out[:, c : c + b.shape[1]] = b[...]
            c += b.shape[1]

    return small_call(
        body, scal, (*backs, dq),
        [pl.BlockSpec(b.shape, lambda j, s: (0, 0)) for b in backs] + [ANY],
        pl.BlockSpec((rows, half), lambda j, s: (0, 1 - s[1])),
        jax.ShapeDtypeStruct(dq.shape, bf16), {len(backs) + 1: 0}, "place_query_grads", 4 * rows * half,
    )


def per_device(queries, key_vectors, value_vectors, out_grad, doc_starts):
    head = lax.axis_index("head")
    core = head % 2
    chip = lax.axis_index("ctx") * 2 + head // 2
    scal = jnp.stack([core * 4, core]).astype(jnp.int32)
    own = assemble(
        scal, key_vectors, value_vectors, core_swapped(key_vectors), core_swapped(value_vectors)
    )
    queries, out_grad, own = lax.optimization_barrier((queries, out_grad, tuple(own)))
    query_other = core_swapped(queries)
    grad_other = core_swapped(out_grad)
    rows = jnp.stack([core, 1 - core])[:, None] * BLK + jnp.arange(BLK)[None, :] + chip * 256
    reached = jnp.where(doc_starts[None, None, :] <= rows[:, :, None], doc_starts[None, None, :], 0)
    first = jnp.max(reached, axis=-1) - (chip * 256 - 512)
    offsets = [sum(CHUNKS[:i]) for i in range(len(CHUNKS))]
    moved = []
    for i, part in enumerate(own):
        if i >= 2:
            moved[i - 2], query_other, grad_other, part = lax.optimization_barrier(
                (moved[i - 2], query_other, grad_other, part)
            )
        moved.append((rolled(part, 4), rolled(part, 2), part))
    dqa = None
    parts = []
    backs = []
    for c0, nk, (y, x, o) in zip(offsets, CHUNKS, moved):
        dqa, dqb, dy, dx, do = chunk(
            scal, first, queries, out_grad, query_other, grad_other, y, x, o, c0, nk, dqa
        )
        if parts:
            parts[-1], dx, dy = lax.optimization_barrier((parts[-1], dx, dy))
        parts.append((do, rolled(dx, -2), rolled(dy, -4)))
        backs.append(core_swapped(dqb))
    grad_query = place_query_grads(scal, dqa, backs)
    sums = None
    for c0, part in zip(offsets, parts):
        sums = add_parts(scal, *part, c0, sums)
    grad_key, grad_value = place_key_grads(scal, sums[0], sums[1], core_swapped(sums[2]))
    return (grad_query, grad_key, grad_value)


def solution(mesh):
    split = P(AXES, None)
    return jax.shard_map(
        per_device,
        mesh=mesh,
        in_specs=(split, split, split, split, P()),
        out_specs=(split, split, split),
        check_vma=False,
    )
```

```python
import functools, math
import jax, jax.numpy as jnp
from jax import lax
from jax.experimental import pallas as pl
from jax.experimental.pallas import tpu as pltpu
from jax.sharding import PartitionSpec as P
HD=128; BLK=128; GRP=8; WIN=640
SCALE=1.0/math.sqrt(HD); LOG2E=1.4426950408889634
TT=(((1,),(1,)),((),()))
NN=(((1,),(0,)),((),()))
TN=(((0,),(0,)),((),()))
f32=jnp.float32; bf16=jnp.bfloat16

def one_set(q,g,dq,off,win,bias,kv,pt,dst,acc,pair):
    K=kv[pl.ds(off,win),0:128]; V=kv[pl.ds(off,win),128:256]; KT=K.T
    b=jnp.concatenate([bias[...]]*pair,axis=1)
    def rows(ref,i):
        return jnp.concatenate([ref[:,(i+u)*HD:(i+u+1)*HD] for u in range(pair)],axis=0)
    def scores(i):
        S=lax.dot_general(K,rows(q,i),TT,preferred_element_type=f32)
        D=lax.dot_general(V,rows(g,i),TT,preferred_element_type=f32)
        return S,D
    ahead=scores(0)
    for i in range(0,GRP,pair):
        S,D=ahead
        if i+pair<GRP: ahead=scores(i+pair)
        u=S*(SCALE*LOG2E)+b
        m=jnp.max(u,axis=0,keepdims=True)
        e=jnp.exp2(u-m)
        l=jnp.sum(e,axis=0,keepdims=True)
        w=jnp.sum(e*D,axis=0,keepdims=True)
        r=1.0/l
        dl=w*r
        Pm=e*r
        dS=(Pm*(D-dl)).astype(bf16)
        pt[0:win,i*HD:(i+pair)*HD]=Pm.astype(bf16)
        dst[0:win,i*HD:(i+pair)*HD]=dS
        dQT=lax.dot_general(KT,dS,NN,preferred_element_type=f32)
        for uu in range(pair):
            dq[:,(i+uu)*HD:(i+uu+1)*HD]=(dQT[:,uu*HD:(uu+1)*HD].T*SCALE).astype(bf16)
    acc[pl.ds(off,win),0:128]+=lax.dot_general(dst[0:win],rows_all(q),NN,preferred_element_type=f32)*SCALE
    acc[pl.ds(off,win),128:256]+=lax.dot_general(pt[0:win],rows_all(g),NN,preferred_element_type=f32)

def rows_all(ref):
    return jnp.concatenate([ref[:,c*HD:(c+1)*HD] for c in range(GRP)],axis=0)

def kernel(scal, first_ref, qa, qb, ga, gb, y_ref, x_ref, o_ref, *rest, pair, mode):
    dqa, dqb, dy, dx, do, kv, bias, pt, dst, acc = rest[-10:]
    j = pl.program_id(0)
    off_a = pl.multiple_of(scal[1]*BLK, BLK)
    off_b = pl.multiple_of((1-scal[1])*BLK, BLK)
    kv[0:256] = y_ref[...]; kv[256:512]=x_ref[...]; kv[512:768]=o_ref[...]
    @pl.when(j==0)
    def _():
        for s, off in ((0,off_a),(1,off_b)):
            t = lax.broadcasted_iota(jnp.int32,(WIN,BLK),0)+off
            p = lax.broadcasted_iota(jnp.int32,(WIN,BLK),1)+off+512
            ok = (t<=p)&(t>=first_ref[s:s+1,:])
            bias[s]=jnp.where(ok,0.0,-1e30).astype(f32)
    acc[...]=jnp.zeros_like(acc)
    for s,(q,g,dq,off) in enumerate(((qa,ga,dqa,off_a),(qb,gb,dqb,off_b))):
        for skip in range(4):
            @pl.when(scal[2+s]==skip)
            def _(s=s,q=q,g=g,dq=dq,off=off,skip=skip):
                one_set(q,g,dq,pl.multiple_of(off+skip*BLK,BLK),WIN-skip*BLK,bias.at[s,pl.ds(skip*BLK,WIN-skip*BLK)],kv,pt,dst,acc,pair)
    dy[...]=acc[0:256].astype(bf16); dx[...]=acc[256:512].astype(bf16); do[...]=acc[512:768]

def chunk(scal, first, q, g, qr, gr, Y, X, O, c0, nk, prev=None, pair=4, mode=0):
    wide=GRP*HD
    own=lambda j,s:(0,s[0]+c0+j)
    oth=lambda j,s:(0,j)
    kvm=lambda j,s:(0,j)
    in_specs=[pl.BlockSpec((2,BLK),lambda j,s:(0,0)),
      pl.BlockSpec((BLK,wide),own),pl.BlockSpec((BLK,wide),own),
      pl.BlockSpec((BLK,wide),own),pl.BlockSpec((BLK,wide),own)]+[pl.BlockSpec((256,256),kvm)]*3
    args=[scal,first,q,qr,g,gr,Y,X,O]
    alias={}
    if prev is not None:
        in_specs+=[pl.BlockSpec(memory_space=pl.ANY)]
        alias={len(args):0}
        args+=[prev]
    out_shape=[jax.ShapeDtypeStruct(q.shape,bf16),jax.ShapeDtypeStruct((BLK,wide*nk),bf16)]+[jax.ShapeDtypeStruct((256,256*nk),bf16)]*2+[jax.ShapeDtypeStruct((256,256*nk),f32)]
    out_specs=[pl.BlockSpec((BLK,wide),own),pl.BlockSpec((BLK,wide),oth)]+[pl.BlockSpec((256,256),kvm)]*3
    return pl.pallas_call(functools.partial(kernel,pair=pair,mode=mode),
      grid_spec=pltpu.PrefetchScalarGridSpec(num_scalar_prefetch=1,grid=(nk,),in_specs=in_specs,out_specs=out_specs,
        scratch_shapes=[pltpu.VMEM((768,256),bf16),pltpu.VMEM((2,WIN,BLK),f32),pltpu.VMEM((WIN,GRP*HD),bf16),pltpu.VMEM((WIN,GRP*HD),bf16),pltpu.VMEM((768,256),f32)]),
      out_shape=out_shape,input_output_aliases=alias,
      compiler_params=pltpu.CompilerParams(vmem_limit_bytes=48*1024*1024,dimension_semantics=("arbitrary",)),
      cost_estimate=pl.CostEstimate(flops=4*nk*2*5*2*1024*640*128,bytes_accessed=nk*2*2**20,transcendentals=0),
      name="band_grads")(*args)


CHUNKS = (2, 2)
LIMIT = 32 * 1024 * 1024
AXES = ("ctx", "head")
ANY = pl.BlockSpec(memory_space=pl.ANY)


def rolled(value, steps):
    count = lax.axis_size("ctx") * lax.axis_size("head")
    return lax.ppermute(value, AXES, [(s, (s + steps) % count) for s in range(count)])


def core_swapped(value):
    count = lax.axis_size("ctx") * lax.axis_size("head")
    return lax.ppermute(value, AXES, [(s, s ^ 1) for s in range(count)])


def small_call(body, scal, args, in_specs, out_specs, out_shape, alias, name, moved):
    return pl.pallas_call(
        body,
        grid_spec=pltpu.PrefetchScalarGridSpec(
            num_scalar_prefetch=1, grid=(1,), in_specs=in_specs, out_specs=out_specs
        ),
        out_shape=out_shape,
        input_output_aliases=alias,
        compiler_params=pltpu.CompilerParams(vmem_limit_bytes=LIMIT),
        cost_estimate=pl.CostEstimate(flops=0, bytes_accessed=moved, transcendentals=0),
        name=name,
    )(scal, *args)


def assemble(scal, key_vectors, value_vectors, key_other, value_other):
    rows, width = key_vectors.shape
    half = width // 2

    def body(s, km, vm, kt, vt, *outs):
        here = pl.multiple_of(s[1] * rows, rows)
        there = pl.multiple_of((1 - s[1]) * rows, rows)
        c = 0
        for nk, out in zip(CHUNKS, outs):
            for i in range(nk):
                for k, v, at in ((km, vm, here), (kt, vt, there)):
                    out[pl.ds(at, rows), 2 * i * HD : (2 * i + 1) * HD] = k[:, c : c + HD]
                    out[pl.ds(at, rows), (2 * i + 1) * HD : (2 * i + 2) * HD] = v[:, c : c + HD]
                c += HD

    own = pl.BlockSpec((rows, half), lambda j, s: (0, s[1]))
    sizes = [2 * HD * nk for nk in CHUNKS]
    return small_call(
        body, scal, (key_vectors, value_vectors, key_other, value_other), [own] * 4,
        [pl.BlockSpec((2 * rows, size), lambda j, s: (0, 0)) for size in sizes],
        [jax.ShapeDtypeStruct((2 * rows, size), bf16) for size in sizes],
        {}, "assemble", 4 * rows * width * 2,
    )


def add_parts(scal, do, rx, ry, c0, prev):
    size = do.shape[1]
    half = 8 * HD // 2

    def body(s, o, x, y, *rest):
        gk, gv, sent = rest[-3:]
        here = pl.multiple_of(s[1] * BLK, BLK)
        there = pl.multiple_of((1 - s[1]) * BLK, BLK)

        def rows(at):
            return (
                o[pl.ds(at, BLK), :] + x[pl.ds(at, BLK), :].astype(f32) + y[pl.ds(at, BLK), :].astype(f32)
            ).astype(bf16)

        sent[...] = rows(there)
        stay = rows(here)
        for c in range(0, size, 2 * HD):
            gk[:, c // 2 : c // 2 + HD] = stay[:, c : c + HD]
            gv[:, c // 2 : c // 2 + HD] = stay[:, c + HD : c + 2 * HD]

    whole = pl.BlockSpec((2 * BLK, size), lambda j, s: (0, 0))
    per = half * 2 // size
    at = c0 * 2 * HD // size
    out_specs = [pl.BlockSpec((BLK, size // 2), lambda j, s: (0, s[1] * per + at))] * 2
    out_specs += [pl.BlockSpec((BLK, size), lambda j, s: (0, at))]
    shape = jax.ShapeDtypeStruct((BLK, 8 * HD), bf16)
    args, in_specs, alias = (do, rx, ry), [whole] * 3, {}
    if prev is not None:
        args, in_specs, alias = args + tuple(prev), in_specs + [ANY] * 3, {4: 0, 5: 1, 6: 2}
    return small_call(
        body, scal, args, in_specs, out_specs, [shape] * 3, alias, "add_parts", 512 * size * 8
    )


def place_key_grads(scal, gk, gv, back):
    rows, width = back.shape
    half = width // 2

    def body(s, b, k_in, v_in, k_out, v_out):
        for c in range(0, half, HD):
            k_out[:, c : c + HD] = b[:, 2 * c : 2 * c + HD]
            v_out[:, c : c + HD] = b[:, 2 * c + HD : 2 * c + 2 * HD]

    other = pl.BlockSpec((rows, half), lambda j, s: (0, 1 - s[1]))
    shape = jax.ShapeDtypeStruct((rows, width), bf16)
    return small_call(
        body, scal, (back, gk, gv), [pl.BlockSpec((rows, width), lambda j, s: (0, 0)), ANY, ANY],
        [other, other], [shape, shape], {2: 0, 3: 1}, "place_key_grads", 4 * rows * width,
    )


def place_query_grads(scal, dq, backs):
    rows, half = dq.shape[0], dq.shape[1] // 2

    def body(s, *refs):
        out = refs[-1]
        c = 0
        for b in refs[:-2]:
            out[:, c : c + b.shape[1]] = b[...]
            c += b.shape[1]

    return small_call(
        body, scal, (*backs, dq),
        [pl.BlockSpec(b.shape, lambda j, s: (0, 0)) for b in backs] + [ANY],
        pl.BlockSpec((rows, half), lambda j, s: (0, 1 - s[1])),
        jax.ShapeDtypeStruct(dq.shape, bf16), {len(backs) + 1: 0}, "place_query_grads", 4 * rows * half,
    )


def per_device(queries, key_vectors, value_vectors, out_grad, doc_starts):
    head = lax.axis_index("head")
    core = head % 2
    chip = lax.axis_index("ctx") * 2 + head // 2
    scal = jnp.stack([core * 4, core]).astype(jnp.int32)
    own = assemble(
        scal, key_vectors, value_vectors, core_swapped(key_vectors), core_swapped(value_vectors)
    )
    queries, out_grad, own = lax.optimization_barrier((queries, out_grad, tuple(own)))
    query_other = core_swapped(queries)
    grad_other = core_swapped(out_grad)
    rows = jnp.stack([core, 1 - core])[:, None] * BLK + jnp.arange(BLK)[None, :] + chip * 256
    reached = jnp.where(doc_starts[None, None, :] <= rows[:, :, None], doc_starts[None, None, :], 0)
    first = jnp.max(reached, axis=-1) - (chip * 256 - 512)
    skips = jnp.clip((first[:, 0] - jnp.stack([core, 1 - core]) * BLK) // BLK, 0, 3)
    band_scal = jnp.concatenate([scal, skips.astype(jnp.int32)])
    offsets = [sum(CHUNKS[:i]) for i in range(len(CHUNKS))]
    moved = []
    for i, part in enumerate(own):
        moved.append((rolled(part, 4), rolled(part, 2), part))
    dqa = None
    parts = []
    backs = []
    for c0, nk, (y, x, o) in zip(offsets, CHUNKS, moved):
        dqa, dqb, dy, dx, do = chunk(
            band_scal, first, queries, out_grad, query_other, grad_other, y, x, o, c0, nk, dqa, pair=4, mode=1
        )
        if parts:
            parts[-1], dx, dy = lax.optimization_barrier((parts[-1], dx, dy))
        parts.append((do, rolled(dx, -2), rolled(dy, -4)))
        backs.append(core_swapped(dqb))
    grad_query = place_query_grads(scal, dqa, backs)
    sums = None
    for c0, part in zip(offsets, parts):
        sums = add_parts(scal, *part, c0, sums)
    grad_key, grad_value = place_key_grads(scal, sums[0], sums[1], core_swapped(sums[2]))
    return (grad_query, grad_key, grad_value)


def solution(mesh):
    split = P(AXES, None)
    return jax.shard_map(
        per_device,
        mesh=mesh,
        in_specs=(split, split, split, split, P()),
        out_specs=(split, split, split),
        check_vma=False,
    )
```

```python
import functools, math
import jax, jax.numpy as jnp
from jax import lax
from jax.experimental import pallas as pl
from jax.experimental.pallas import tpu as pltpu
from jax.sharding import PartitionSpec as P
HD=128; BLK=128; GRP=8; WIN=640
SCALE=1.0/math.sqrt(HD); LOG2E=1.4426950408889634
TT=(((1,),(1,)),((),()))
NN=(((1,),(0,)),((),()))
TN=(((0,),(0,)),((),()))
f32=jnp.float32; bf16=jnp.bfloat16

def one_set(q,g,dq,off,win,bias,kv,pt,dst,acc,pair):
    K=kv[pl.ds(off,win),0:128]; V=kv[pl.ds(off,win),128:256]; KT=K.T
    b=jnp.concatenate([bias[...]]*pair,axis=1)
    def rows(ref,i):
        return jnp.concatenate([ref[:,(i+u)*HD:(i+u+1)*HD] for u in range(pair)],axis=0)
    def scores(i):
        S=lax.dot_general(K,rows(q,i),TT,preferred_element_type=f32)
        D=lax.dot_general(V,rows(g,i),TT,preferred_element_type=f32)
        return S,D
    ahead=scores(0)
    for i in range(0,GRP,pair):
        S,D=ahead
        if i+pair<GRP: ahead=scores(i+pair)
        u=S*(SCALE*LOG2E)+b
        m=jnp.max(u,axis=0,keepdims=True)
        e=jnp.exp2(u-m)
        l=jnp.sum(e,axis=0,keepdims=True)
        w=jnp.sum(e*D,axis=0,keepdims=True)
        r=1.0/l
        dl=w*r
        Pm=e*r
        dS=(Pm*(D-dl)).astype(bf16)
        pt[0:win,i*HD:(i+pair)*HD]=Pm.astype(bf16)
        dst[0:win,i*HD:(i+pair)*HD]=dS
        dQT=lax.dot_general(KT,dS,NN,preferred_element_type=f32)
        for uu in range(pair):
            dq[:,(i+uu)*HD:(i+uu+1)*HD]=(dQT[:,uu*HD:(uu+1)*HD].T*SCALE).astype(bf16)
    acc[pl.ds(off,win),0:128]+=lax.dot_general(dst[0:win],rows_all(q),NN,preferred_element_type=f32)*SCALE
    acc[pl.ds(off,win),128:256]+=lax.dot_general(pt[0:win],rows_all(g),NN,preferred_element_type=f32)

def rows_all(ref):
    return jnp.concatenate([ref[:,c*HD:(c+1)*HD] for c in range(GRP)],axis=0)

def kernel(scal, first_ref, qa, qb, ga, gb, y_ref, x_ref, o_ref, *rest, pair, mode):
    dqa, dqb, dy, dx, do, kv, bias, pt, dst, acc = rest[-10:]
    j = pl.program_id(0)
    off_a = pl.multiple_of(scal[1]*BLK, BLK)
    off_b = pl.multiple_of((1-scal[1])*BLK, BLK)
    kv[0:256] = y_ref[...]; kv[256:512]=x_ref[...]; kv[512:768]=o_ref[...]
    @pl.when(j==0)
    def _():
        for s, off in ((0,off_a),(1,off_b)):
            t = lax.broadcasted_iota(jnp.int32,(WIN,BLK),0)+off
            p = lax.broadcasted_iota(jnp.int32,(WIN,BLK),1)+off+512
            ok = (t<=p)&(t>=first_ref[s:s+1,:])
            bias[s]=jnp.where(ok,0.0,-1e30).astype(f32)
    acc[...]=jnp.zeros_like(acc)
    for s,(q,g,dq,off) in enumerate(((qa,ga,dqa,off_a),(qb,gb,dqb,off_b))):
        for skip in range(4):
            @pl.when(scal[2+s]==skip)
            def _(s=s,q=q,g=g,dq=dq,off=off,skip=skip):
                one_set(q,g,dq,pl.multiple_of(off+skip*BLK,BLK),WIN-skip*BLK,bias.at[s,pl.ds(skip*BLK,WIN-skip*BLK)],kv,pt,dst,acc,pair)
    dy[...]=acc[0:256].astype(bf16); dx[...]=acc[256:512].astype(bf16); do[...]=acc[512:768]

def chunk(scal, first, q, g, qr, gr, Y, X, O, c0, nk, prev=None, pair=4, mode=0):
    wide=GRP*HD
    own=lambda j,s:(0,s[0]+c0+j)
    oth=lambda j,s:(0,j)
    kvm=lambda j,s:(0,j)
    in_specs=[pl.BlockSpec((2,BLK),lambda j,s:(0,0)),
      pl.BlockSpec((BLK,wide),own),pl.BlockSpec((BLK,wide),own),
      pl.BlockSpec((BLK,wide),own),pl.BlockSpec((BLK,wide),own)]+[pl.BlockSpec((256,256),kvm)]*3
    args=[scal,first,q,qr,g,gr,Y,X,O]
    alias={}
    if prev is not None:
        in_specs+=[pl.BlockSpec(memory_space=pl.ANY)]
        alias={len(args):0}
        args+=[prev]
    out_shape=[jax.ShapeDtypeStruct(q.shape,bf16),jax.ShapeDtypeStruct((BLK,wide*nk),bf16)]+[jax.ShapeDtypeStruct((256,256*nk),bf16)]*2+[jax.ShapeDtypeStruct((256,256*nk),f32)]
    out_specs=[pl.BlockSpec((BLK,wide),own),pl.BlockSpec((BLK,wide),oth)]+[pl.BlockSpec((256,256),kvm)]*3
    return pl.pallas_call(functools.partial(kernel,pair=pair,mode=mode),
      grid_spec=pltpu.PrefetchScalarGridSpec(num_scalar_prefetch=1,grid=(nk,),in_specs=in_specs,out_specs=out_specs,
        scratch_shapes=[pltpu.VMEM((768,256),bf16),pltpu.VMEM((2,WIN,BLK),f32),pltpu.VMEM((WIN,GRP*HD),bf16),pltpu.VMEM((WIN,GRP*HD),bf16),pltpu.VMEM((768,256),f32)]),
      out_shape=out_shape,input_output_aliases=alias,
      compiler_params=pltpu.CompilerParams(vmem_limit_bytes=48*1024*1024,dimension_semantics=("arbitrary",)),
      cost_estimate=pl.CostEstimate(flops=4*nk*2*5*2*1024*640*128,bytes_accessed=nk*2*2**20,transcendentals=0),
      name="band_grads")(*args)


CHUNKS = (2, 2)
LIMIT = 32 * 1024 * 1024
AXES = ("ctx", "head")
ANY = pl.BlockSpec(memory_space=pl.ANY)


def rolled(value, steps):
    count = lax.axis_size("ctx") * lax.axis_size("head")
    return lax.ppermute(value, AXES, [(s, (s + steps) % count) for s in range(count)])


def core_swapped(value):
    count = lax.axis_size("ctx") * lax.axis_size("head")
    return lax.ppermute(value, AXES, [(s, s ^ 1) for s in range(count)])


def small_call(body, scal, args, in_specs, out_specs, out_shape, alias, name, moved):
    return pl.pallas_call(
        body,
        grid_spec=pltpu.PrefetchScalarGridSpec(
            num_scalar_prefetch=1, grid=(1,), in_specs=in_specs, out_specs=out_specs
        ),
        out_shape=out_shape,
        input_output_aliases=alias,
        compiler_params=pltpu.CompilerParams(vmem_limit_bytes=LIMIT),
        cost_estimate=pl.CostEstimate(flops=0, bytes_accessed=moved, transcendentals=0),
        name=name,
    )(scal, *args)


def assemble(scal, key_vectors, value_vectors, key_other, value_other):
    rows, width = key_vectors.shape
    half = width // 2

    def body(s, km, vm, kt, vt, *outs):
        here = pl.multiple_of(s[1] * rows, rows)
        there = pl.multiple_of((1 - s[1]) * rows, rows)
        c = 0
        for nk, out in zip(CHUNKS, outs):
            for i in range(nk):
                for k, v, at in ((km, vm, here), (kt, vt, there)):
                    out[pl.ds(at, rows), 2 * i * HD : (2 * i + 1) * HD] = k[:, c : c + HD]
                    out[pl.ds(at, rows), (2 * i + 1) * HD : (2 * i + 2) * HD] = v[:, c : c + HD]
                c += HD

    own = pl.BlockSpec((rows, half), lambda j, s: (0, s[1]))
    sizes = [2 * HD * nk for nk in CHUNKS]
    return small_call(
        body, scal, (key_vectors, value_vectors, key_other, value_other), [own] * 4,
        [pl.BlockSpec((2 * rows, size), lambda j, s: (0, 0)) for size in sizes],
        [jax.ShapeDtypeStruct((2 * rows, size), bf16) for size in sizes],
        {}, "assemble", 4 * rows * width * 2,
    )


def add_parts(scal, do, rx, ry, c0, prev):
    size = do.shape[1]
    half = 8 * HD // 2

    def body(s, o, x, y, *rest):
        gk, gv, sent = rest[-3:]
        here = pl.multiple_of(s[1] * BLK, BLK)
        there = pl.multiple_of((1 - s[1]) * BLK, BLK)

        def rows(at):
            return (
                o[pl.ds(at, BLK), :] + x[pl.ds(at, BLK), :].astype(f32) + y[pl.ds(at, BLK), :].astype(f32)
            ).astype(bf16)

        sent[...] = rows(there)
        stay = rows(here)
        for c in range(0, size, 2 * HD):
            gk[:, c // 2 : c // 2 + HD] = stay[:, c : c + HD]
            gv[:, c // 2 : c // 2 + HD] = stay[:, c + HD : c + 2 * HD]

    whole = pl.BlockSpec((2 * BLK, size), lambda j, s: (0, 0))
    per = half * 2 // size
    at = c0 * 2 * HD // size
    out_specs = [pl.BlockSpec((BLK, size // 2), lambda j, s: (0, s[1] * per + at))] * 2
    out_specs += [pl.BlockSpec((BLK, size), lambda j, s: (0, at))]
    shape = jax.ShapeDtypeStruct((BLK, 8 * HD), bf16)
    args, in_specs, alias = (do, rx, ry), [whole] * 3, {}
    if prev is not None:
        args, in_specs, alias = args + tuple(prev), in_specs + [ANY] * 3, {4: 0, 5: 1, 6: 2}
    return small_call(
        body, scal, args, in_specs, out_specs, [shape] * 3, alias, "add_parts", 512 * size * 8
    )


def place_key_grads(scal, gk, gv, back):
    rows, width = back.shape
    half = width // 2

    def body(s, b, k_in, v_in, k_out, v_out):
        for c in range(0, half, HD):
            k_out[:, c : c + HD] = b[:, 2 * c : 2 * c + HD]
            v_out[:, c : c + HD] = b[:, 2 * c + HD : 2 * c + 2 * HD]

    other = pl.BlockSpec((rows, half), lambda j, s: (0, 1 - s[1]))
    shape = jax.ShapeDtypeStruct((rows, width), bf16)
    return small_call(
        body, scal, (back, gk, gv), [pl.BlockSpec((rows, width), lambda j, s: (0, 0)), ANY, ANY],
        [other, other], [shape, shape], {2: 0, 3: 1}, "place_key_grads", 4 * rows * width,
    )


def place_query_grads(scal, dq, backs):
    rows, half = dq.shape[0], dq.shape[1] // 2

    def body(s, *refs):
        out = refs[-1]
        c = 0
        for b in refs[:-2]:
            out[:, c : c + b.shape[1]] = b[...]
            c += b.shape[1]

    return small_call(
        body, scal, (*backs, dq),
        [pl.BlockSpec(b.shape, lambda j, s: (0, 0)) for b in backs] + [ANY],
        pl.BlockSpec((rows, half), lambda j, s: (0, 1 - s[1])),
        jax.ShapeDtypeStruct(dq.shape, bf16), {len(backs) + 1: 0}, "place_query_grads", 4 * rows * half,
    )


def per_device(queries, key_vectors, value_vectors, out_grad, doc_starts):
    head = lax.axis_index("head")
    core = head % 2
    chip = lax.axis_index("ctx") * 2 + head // 2
    scal = jnp.stack([core * 4, core]).astype(jnp.int32)
    own = assemble(
        scal, key_vectors, value_vectors, core_swapped(key_vectors), core_swapped(value_vectors)
    )
    queries, out_grad, own = lax.optimization_barrier((queries, out_grad, tuple(own)))
    query_other = core_swapped(queries)
    grad_other = core_swapped(out_grad)
    doc_starts, query_other, grad_other = lax.optimization_barrier(
        (doc_starts, query_other, grad_other)
    )
    rows = jnp.stack([core, 1 - core])[:, None] * BLK + jnp.arange(BLK)[None, :] + chip * 256
    reached = jnp.where(doc_starts[None, None, :] <= rows[:, :, None], doc_starts[None, None, :], 0)
    first = jnp.max(reached, axis=-1) - (chip * 256 - 512)
    skips = jnp.clip((first[:, 0] - jnp.stack([core, 1 - core]) * BLK) // BLK, 0, 3)
    band_scal = jnp.concatenate([scal, skips.astype(jnp.int32)])
    offsets = [sum(CHUNKS[:i]) for i in range(len(CHUNKS))]
    moved = []
    for i, part in enumerate(own):
        moved.append((rolled(part, 4), rolled(part, 2), part))
    dqa = None
    parts = []
    backs = []
    for c0, nk, (y, x, o) in zip(offsets, CHUNKS, moved):
        dqa, dqb, dy, dx, do = chunk(
            band_scal, first, queries, out_grad, query_other, grad_other, y, x, o, c0, nk, dqa, pair=4, mode=1
        )
        if parts:
            parts[-1], dx, dy = lax.optimization_barrier((parts[-1], dx, dy))
        parts.append((do, rolled(dx, -2), rolled(dy, -4)))
        backs.append(core_swapped(dqb))
    grad_query = place_query_grads(scal, dqa, backs)
    sums = None
    for c0, part in zip(offsets, parts):
        sums = add_parts(scal, *part, c0, sums)
    grad_key, grad_value = place_key_grads(scal, sums[0], sums[1], core_swapped(sums[2]))
    return (grad_query, grad_key, grad_value)


def solution(mesh):
    split = P(AXES, None)
    return jax.shard_map(
        per_device,
        mesh=mesh,
        in_specs=(split, split, split, split, P()),
        out_specs=(split, split, split),
        check_vma=False,
    )
```
